32 devices in a mesh: grp: 8 (over z, core), head: 4 (over y, x).
Axes of the slice: x: 2, y: 2, z: 4, core: 2. Of those that a mesh axis runs over, the one named last changes fastest.
Arguments:
- res_cache: bfloat16 [32, 128, 576], P('grp'), may hold values from -6 to 6, as said below
- res_lengths: int32 [32], P('grp'), may hold values from 2 to 128, as said below
- res_query: bfloat16 [32, 16, 576], P('grp', 'head'), may hold values from -40 to 40
- new_cache: bfloat16 [8, 2048, 576], P(None, ('grp', 'head')), may hold values from -6 to 6, as said below
- new_lengths: int32 [8], replicated, may hold values from 2 to 2048, as said below
- assignment: int32 [8], replicated, may hold values from 0 to 7, each once
- new_query: bfloat16 [8, 16, 576], P('grp', 'head'), may hold values from -40 to 40
- value_up_weight: bfloat16 [16, 512, 128], P('head'), may hold values from -1.5 to 1.5
- w_out: bfloat16 [2048, 3584], P('head'), may hold values from -0.125 to 0.125
Outputs:
- res_mixed: bfloat16 [32, 3584], P('grp')
- new_mixed: bfloat16 [8, 3584], P('grp')
The draws below stay inside these ranges and needn't reach their ends.
Inputs may be any that keep to these rules, and one draw needn't show every extreme that they name: `res_cache`: tokens of a cache may differ in scale. `res_lengths`: at least 2, and some row reaches 128. `new_cache`: tokens of a cache may differ in scale. `new_lengths`: at least 2, and some request reaches 2048. `assignment`: every group serves exactly one request.
All inputs are finite; a program needn't handle non-finite values.
Results may differ from the reference program's by a relative error of at most 0.012.
Values may be sent and summed in bfloat16 or wider, within the bound.
A program may use at most 128 MiB of HBM per device.

```python
import jax
import jax.numpy as jnp
from jax import lax

D = 3584
LATENT_WIDTH = 512
VALUE_HEAD_WIDTH = 128
L_RES = 128
HEAD_TOTAL = 16
LATENT = 576
LP = 2048
ROWS_RES = 32
N_GRP = 8


def drawn_field(key, field_shape):
    return jnp.clip(jax.random.normal(key, field_shape), -6.0, 6.0)


def draw_res_cache(key, part):
    key = jax.random.fold_in(key, 11)
    return drawn_field(key, (ROWS_RES, L_RES, LATENT)).astype(jnp.bfloat16)


def draw_new_cache(key, part):
    key = jax.random.fold_in(key, 12)
    return drawn_field(key, (N_GRP, LP, LATENT)).astype(jnp.bfloat16)


def draw_res_query(key, part):
    key = jax.random.fold_in(key, 21)
    return drawn_field(key, (ROWS_RES, HEAD_TOTAL, LATENT)).astype(jnp.bfloat16)


def draw_new_query(key, part):
    key = jax.random.fold_in(key, 22)
    return drawn_field(key, (N_GRP, HEAD_TOTAL, LATENT)).astype(jnp.bfloat16)


def draw_res_lengths(key, part):
    key = jax.random.fold_in(key, 31)
    lengths = jax.random.randint(key, (ROWS_RES,), 2, L_RES + 1)
    return lengths.at[0].set(L_RES).astype(jnp.int32)


def draw_new_lengths(key, part):
    key = jax.random.fold_in(key, 32)
    lengths = jax.random.randint(key, (N_GRP,), 2, LP + 1)
    return lengths.at[0].set(LP).astype(jnp.int32)


def level_of(stream_key, extent, shards, low, high):
    loudness = 1.0
    for position, shards_of in shards:
        steps = jax.random.uniform(jax.random.fold_in(jax.random.fold_in(stream_key, 6), position), (shards_of,), jnp.float32, low / len(shards), high / len(shards))
        loudness = loudness * jnp.repeat(jnp.exp(steps), extent[position] // shards_of).reshape((-1,) + (1,) * (len(extent) - 1 - position))
    return loudness


def scatter_about(stream_key, shape, width, bound, pieces=(), kind=jnp.bfloat16):
    values = width * jax.random.normal(stream_key, shape, jnp.float32)
    if pieces:
        values = values * level_of(stream_key, shape, pieces, -0.22, 0.18)
    return jnp.clip(values, -bound, bound).astype(kind)


def setup_inputs(seed: int = 0) -> dict:
    splits = jax.random.split(jax.random.key(seed), 10)
    res_cache = draw_res_cache(jax.random.fold_in(splits[9], 71), 0)
    res_lengths = draw_res_lengths(jax.random.fold_in(splits[9], 71), 0)
    res_query = draw_res_query(jax.random.fold_in(splits[9], 71), 0)
    new_cache = draw_new_cache(jax.random.fold_in(splits[9], 71), 0)
    new_lengths = draw_new_lengths(jax.random.fold_in(splits[9], 71), 0)
    assignment = jax.random.permutation(splits[5], N_GRP).astype(jnp.int32)
    new_query = draw_new_query(jax.random.fold_in(splits[9], 71), 0)
    value_up_weight = scatter_about(splits[7], (HEAD_TOTAL, LATENT_WIDTH, VALUE_HEAD_WIDTH), (LATENT_WIDTH // 32) ** -0.5, 1.5, ((0, 4),))
    w_out = scatter_about(splits[8], (HEAD_TOTAL * VALUE_HEAD_WIDTH, D), (HEAD_TOTAL * VALUE_HEAD_WIDTH) ** -0.5, 0.125, ((0, 4),))
    return {"res_cache": res_cache, "res_lengths": res_lengths, "res_query": res_query, "new_cache": new_cache, "new_lengths": new_lengths, "assignment": assignment, "new_query": new_query, "value_up_weight": value_up_weight, "w_out": w_out}


score_scale = 192.0 ** -0.5
neg_large = -1.0e30


def attend(queries, latent_key_rows, usable):
    scores = jnp.dot(queries, latent_key_rows.T, preferred_element_type=jnp.float32) * score_scale
    scores = jnp.where(usable[None, :], scores, neg_large)
    running_max = jnp.max(scores, axis=1, keepdims=True)
    attention_weights = jnp.where(usable[None, :], jnp.exp(scores - running_max), 0.0)
    weight_sum = jnp.sum(attention_weights, axis=1, keepdims=True)
    latent_vector = jnp.dot(attention_weights.astype(jnp.bfloat16), latent_key_rows[:, :LATENT_WIDTH], preferred_element_type=jnp.float32)
    return (latent_vector / weight_sum).astype(jnp.bfloat16)


def project(latent_vector, value_up_weight, w_out):
    per_head_values = jnp.einsum("dic,icn->din", latent_vector.astype(jnp.float32), value_up_weight.astype(jnp.float32)).astype(jnp.bfloat16)
    head_rows = per_head_values.reshape(latent_vector.shape[0], HEAD_TOTAL * VALUE_HEAD_WIDTH)
    return jnp.dot(head_rows, w_out, preferred_element_type=jnp.float32).astype(jnp.bfloat16)


def reference(res_cache, res_lengths, res_query, new_cache, new_lengths, assignment, new_query, value_up_weight, w_out):
    res_slots = jnp.arange(L_RES, dtype=jnp.int32)

    def resident_row(row_items):
        queries, latent_key_rows, length = row_items
        return attend(queries, latent_key_rows, res_slots < length)

    res_latent = lax.map(resident_row, (res_query, res_cache, res_lengths))
    group_slots = jnp.arange(N_GRP, dtype=jnp.int32)
    inverse = jnp.sum(jnp.where(assignment[:, None] == group_slots[None, :], group_slots[:, None], 0), axis=0).astype(jnp.int32)
    token_slots = jnp.arange(LP, dtype=jnp.int32)

    def served_row(row_items):
        queries, request = row_items
        return attend(queries, new_cache[request], token_slots < new_lengths[request])

    new_latent = lax.map(served_row, (new_query, inverse))
    return project(res_latent, value_up_weight, w_out), project(new_latent, value_up_weight, w_out)
```

```python
import functools

import jax
import jax.numpy as jnp
from jax import lax
from jax.experimental import pallas as pl
from jax.experimental.pallas import tpu as pltpu
from jax.sharding import PartitionSpec as P

score_scale = 192.0 ** (-0.5)
neg_large = -1e30
F32 = jnp.float32
BF16 = jnp.bfloat16
MESH = pl.DeviceIdType.MESH


def for_each(low, high, body):
    if high - low <= 4:
        for i in range(low, high):
            body(i)
    else:
        lax.fori_loop(low, high, lambda i, c: (body(i), c)[1], 0)


def attend(queries, tokens, mask, width):
    scores = (
        lax.dot_general(
            queries, tokens, (((1,), (1,)), ((), ())), preferred_element_type=F32
        )
        * score_scale
    )
    scores = jnp.where(mask, scores, neg_large)
    top = jnp.max(scores, axis=1, keepdims=True)
    top_hi = top.astype(BF16).astype(F32)
    rest = top - top_hi
    top_lo = (rest + jnp.abs(rest) * (2.0**-7)).astype(BF16).astype(F32)
    bound = top_hi + top_lo
    weights = jnp.where(mask, jnp.exp(scores - bound), 0.0)
    total = jnp.sum(weights, axis=1, keepdims=True)
    weighted = jnp.dot(
        weights.astype(BF16), tokens[:, :width], preferred_element_type=F32
    )
    return top_hi, top_lo, total, weighted


def up_project(latent, up_ref, heads):
    rows = latent.shape[0]
    head_of_row = lax.broadcasted_iota(jnp.int32, (rows, 1), 0) % heads
    out = None
    for head in range(heads):
        part = jnp.dot(latent, up_ref[head], preferred_element_type=F32)
        part = jnp.where(head_of_row == head, part, 0.0)
        out = part if out is None else out + part
    return out


def flatten_heads(values, heads):
    rows, width = values.shape
    head_of_row = lax.broadcasted_iota(jnp.int32, (rows, 1), 0) % heads
    wide = jnp.concatenate(
        [jnp.where(head_of_row == head, values, 0.0) for head in range(heads)], axis=1
    )
    return jnp.sum(wide.reshape(rows // heads, heads, heads * width), axis=1)


def kernel(
    n_grp,
    n_head,
    res_lengths,
    new_lengths,
    assignment,
    res_cache_hbm,
    res_query_hbm,
    new_cache_hbm,
    new_query_hbm,
    up_hbm,
    w_out_hbm,
    res_out,
    new_out,
    res_cache,
    res_query,
    new_cache,
    up,
    w_out,
    q_in,
    q_all,
    rep_out,
    rep_in,
    val_out,
    val_in,
    res_part,
    new_part,
    load_sem,
    r1_send,
    r1_recv,
    r2_send,
    r2_recv,
    r3_send,
    r3_recv,
    r4_send,
    r4_recv,
    r5_send,
    r5_recv,
    r6_send,
    r6_recv,
):
    grp = lax.axis_index("grp")
    head = lax.axis_index("head")
    residents, slots, latent = res_cache.shape
    heads = up.shape[0]
    width = up.shape[1]
    head_width = up.shape[2]
    requests, shard, _ = new_cache.shape
    features = w_out.shape[1]
    block_rows = n_grp * heads
    tokens = requests * shard
    splits = res_part.shape[1] // residents
    piece = features // splits

    loads = [
        pltpu.make_async_copy(src, dst, load_sem.at[i])
        for i, (src, dst) in enumerate(
            (
                (new_query_hbm.at[0], q_in.at[0]),
                (res_query_hbm, res_query),
                (res_cache_hbm, res_cache),
                (up_hbm, up),
                (new_cache_hbm, new_cache),
                (w_out_hbm, w_out),
            )
        )
    ]
    for load in loads:
        load.start()
    load_q, load_res_q, load_res, load_up, load_new, load_w = loads

    def grp_at(off):
        return lax.rem(grp + off, n_grp)

    def head_at(off):
        return lax.rem(head + off, n_head)

    barrier = pltpu.get_barrier_semaphore()

    def greet_grp(off):
        pl.semaphore_signal(
            barrier, inc=1, device_id=(grp_at(off), head), device_id_type=MESH
        )

    def greet_head(off):
        pl.semaphore_signal(
            barrier, inc=1, device_id=(grp, head_at(off)), device_id_type=MESH
        )

    for_each(1, n_grp, greet_grp)
    for_each(1, n_head, greet_head)

    def r1(off):
        return pltpu.make_async_remote_copy(
            src_ref=new_query_hbm.at[0],
            dst_ref=q_in.at[off],
            send_sem=r1_send.at[off],
            recv_sem=r1_recv.at[off],
            device_id=(grp_at(off), head),
            device_id_type=MESH,
        )

    def r2(off):
        return pltpu.make_async_remote_copy(
            src_ref=q_all.at[0],
            dst_ref=q_all.at[off],
            send_sem=r2_send.at[off],
            recv_sem=r2_recv.at[off],
            device_id=(grp, head_at(off)),
            device_id_type=MESH,
        )

    def r3(off):
        return pltpu.make_async_remote_copy(
            src_ref=rep_out.at[off],
            dst_ref=rep_in.at[off],
            send_sem=r3_send.at[off],
            recv_sem=r3_recv.at[off],
            device_id=(grp, head_at(n_head - off)),
            device_id_type=MESH,
        )

    def r4(off):
        return pltpu.make_async_remote_copy(
            src_ref=val_out.at[off],
            dst_ref=val_in.at[off],
            send_sem=r4_send.at[off],
            recv_sem=r4_recv.at[off],
            device_id=(grp_at(n_grp - off), head),
            device_id_type=MESH,
        )

    def r5(off):
        return pltpu.make_async_remote_copy(
            src_ref=res_part.at[head],
            dst_ref=res_part.at[head],
            send_sem=r5_send.at[off],
            recv_sem=r5_recv.at[off],
            device_id=(grp, head_at(off)),
            device_id_type=MESH,
        )

    def r6(off):
        return pltpu.make_async_remote_copy(
            src_ref=new_part.at[head],
            dst_ref=new_part.at[head],
            send_sem=r6_send.at[off],
            recv_sem=r6_recv.at[off],
            device_id=(grp, head_at(off)),
            device_id_type=MESH,
        )

    pl.semaphore_wait(barrier, n_grp - 1 + n_head - 1)
    for_each(1, n_grp, lambda off: r1(off).start())

    token = lax.broadcasted_iota(jnp.int32, (1, residents * slots), 1)
    row = lax.broadcasted_iota(jnp.int32, (residents * heads, 1), 0) // heads
    live = jnp.full((1, residents * slots), -1, jnp.int32)
    for r in range(residents):
        here = (token >= r * slots) & (token < r * slots + res_lengths[r])
        live = jnp.where(here, r, live)
    load_res_q.wait()
    load_res.wait()
    _, _, res_total, res_weighted = attend(
        res_query[...].astype(F32).reshape(residents * heads, latent).astype(BF16),
        res_cache[...].reshape(residents * slots, latent),
        row == live,
        width,
    )
    res_latent = (res_weighted / res_total).astype(BF16)
    load_up.wait()
    res_values = up_project(res_latent, up, heads).astype(BF16).astype(F32)
    res_rows = flatten_heads(res_values, heads).astype(BF16)

    first = (grp * n_head + head) * shard
    token = lax.broadcasted_iota(jnp.int32, (1, tokens), 1)
    asks = jnp.full((1, tokens), -1, jnp.int32)
    for k in range(requests):
        here = (token >= k * shard) & (token < k * shard + (new_lengths[k] - first))
        here = here & (token < (k + 1) * shard)
        asks = jnp.where(here, assignment[k], asks)
    row = lax.broadcasted_iota(jnp.int32, (block_rows, 1), 0) // heads
    group = grp - row
    group = jnp.where(group < 0, group + n_grp, group)
    mask = group == asks

    load_q.wait()
    for_each(1, n_grp, lambda off: r1(off).wait_recv())
    q_all[0] = q_in[...].astype(F32).reshape(block_rows, latent).astype(BF16)
    for_each(1, n_head, lambda off: r2(off).start())

    load_new.wait()

    def partials(off):
        return attend(
            q_all[off], new_cache[...].reshape(tokens, latent), mask, width
        )

    own_hi, own_lo, own_total, own_weighted = partials(0)

    lane = lax.broadcasted_iota(jnp.int32, (block_rows, 128), 1)

    def answer(off):
        r2(off).wait_recv()
        top_hi, top_lo, total, weighted = partials(off)
        total_hi = total.astype(BF16).astype(F32)
        stats = jnp.where(
            lane < 64,
            jnp.where(lane < 32, top_hi, top_lo),
            jnp.where(lane < 96, total_hi, total - total_hi),
        )
        rep_out[off] = jnp.concatenate([weighted, stats], axis=1).astype(BF16)
        r3(off).start()

    for_each(1, n_head, answer)

    load_w.wait()
    res_partial = jnp.dot(res_rows, w_out[...], preferred_element_type=F32)
    res_part[head] = jnp.concatenate(
        [res_partial[:, i * piece : (i + 1) * piece] for i in range(splits)], axis=0
    ).astype(BF16)
    for_each(1, n_head, lambda off: r5(off).start())

    for_each(1, n_head, lambda off: r3(off).wait_recv())
    tops = [own_hi + own_lo]
    totals = [own_total]
    for off in range(1, n_head):
        stats = rep_in[off, :, width:].astype(F32)
        tops.append(stats[:, 0:1] + stats[:, 32:33])
        totals.append(stats[:, 64:65] + stats[:, 96:97])
    top = functools.reduce(jnp.maximum, tops)
    share = jnp.exp(tops[0] - top)
    total = share * totals[0]
    summed = share * own_weighted
    for off in range(1, n_head):
        share = jnp.exp(tops[off] - top)
        total = total + share * totals[off]
        summed = summed + share * rep_in[off, :, :width].astype(F32)
    values = up_project(summed.astype(BF16), up, heads)
    lane = lax.broadcasted_iota(jnp.int32, (block_rows, 128), 1)
    stats = jnp.where(lane < 64, top, total)
    val_out[...] = jnp.concatenate([values, stats], axis=1).reshape(val_out.shape)
    for_each(1, n_grp, lambda off: r4(off).start())
    val_in[0] = val_out[0]

    for_each(1, n_head, lambda off: r5(off).wait_recv())
    res_sum = res_part[0].astype(F32)
    for rank in range(1, n_head):
        res_sum = res_sum + res_part[rank].astype(F32)
    for i in range(splits):
        res_out[:, i * piece : (i + 1) * piece] = res_sum[
            i * residents : (i + 1) * residents
        ].astype(BF16)

    for_each(1, n_grp, lambda off: r4(off).wait_recv())
    parts = val_in[...]
    tops = parts[:, :, head_width : head_width + 1]
    totals = parts[:, :, head_width + 64 : head_width + 65]
    top = jnp.max(tops, axis=0, keepdims=True)
    share = jnp.exp(tops - top)
    total = jnp.sum(share * totals, axis=0)
    values = jnp.sum(share * parts[:, :, :head_width], axis=0)
    values = (values / total).astype(BF16).astype(F32)
    new_row = flatten_heads(values, heads).astype(BF16)
    new_part[head] = jnp.dot(new_row, w_out[...], preferred_element_type=F32)
    for_each(1, n_head, lambda off: r6(off).start())
    for_each(1, n_head, lambda off: r6(off).wait_recv())
    new_sum = new_part[0]
    for rank in range(1, n_head):
        new_sum = new_sum + new_part[rank]
    new_out[...] = new_sum.astype(BF16)

    for_each(1, n_grp, lambda off: r1(off).wait_send())
    for_each(1, n_head, lambda off: r2(off).wait_send())
    for_each(1, n_head, lambda off: r3(off).wait_send())
    for_each(1, n_grp, lambda off: r4(off).wait_send())
    for_each(1, n_head, lambda off: r5(off).wait_send())
    for_each(1, n_head, lambda off: r6(off).wait_send())


def per_device(
    res_cache,
    res_lengths,
    res_query,
    new_cache,
    new_lengths,
    assignment,
    new_query,
    value_up_weight,
    w_out,
):
    n_grp = lax.axis_size("grp")
    n_head = lax.axis_size("head")
    residents = res_cache.shape[0]
    heads, width, head_width = value_up_weight.shape
    latent = res_cache.shape[2]
    features = w_out.shape[1]
    block_rows = n_grp * heads
    splits = 16 // residents
    smem = pl.BlockSpec(memory_space=pltpu.SMEM)
    anywhere = pl.BlockSpec(memory_space=pl.ANY)
    vmem = pl.BlockSpec(memory_space=pltpu.VMEM)
    dma = pltpu.SemaphoreType.DMA
    grp_sems = [dma((n_grp,)), dma((n_grp,))]
    head_sems = [dma((n_head,)), dma((n_head,))]
    return pl.pallas_call(
        functools.partial(kernel, n_grp, n_head),
        out_shape=(
            jax.ShapeDtypeStruct((residents, features), BF16),
            jax.ShapeDtypeStruct((1, features), BF16),
        ),
        in_specs=[smem] * 3 + [anywhere] * 6,
        out_specs=(vmem, vmem),
        scratch_shapes=[
            pltpu.VMEM(res_cache.shape, BF16),
            pltpu.VMEM(res_query.shape, BF16),
            pltpu.VMEM(new_cache.shape, BF16),
            pltpu.VMEM(value_up_weight.shape, BF16),
            pltpu.VMEM(w_out.shape, BF16),
            pltpu.VMEM((n_grp, heads, latent), BF16),
            pltpu.VMEM((n_head, block_rows, latent), BF16),
            pltpu.VMEM((n_head, block_rows, width + 128), BF16),
            pltpu.VMEM((n_head, block_rows, width + 128), BF16),
            pltpu.VMEM((n_grp, heads, head_width + 128), F32),
            pltpu.VMEM((n_grp, heads, head_width + 128), F32),
            pltpu.VMEM((n_head, residents * splits, features // splits), BF16),
            pltpu.VMEM((n_head, 1, features), F32),
            dma((6,)),
        ]
        + grp_sems
        + head_sems * 2
        + grp_sems
        + head_sems * 2,
        compiler_params=pltpu.CompilerParams(
            collective_id=0, has_side_effects=True, vmem_limit_bytes=48 * 2**20
        ),
    )(
        res_lengths,
        new_lengths,
        assignment,
        res_cache,
        res_query,
        new_cache,
        new_query,
        value_up_weight,
        w_out,
    )


def solution(mesh):
    in_specs = (
        P("grp", None, None),
        P("grp"),
        P("grp", "head", None),
        P(None, ("grp", "head"), None),
        P(),
        P(),
        P("grp", "head", None),
        P("head", None, None),
        P("head", None),
    )
    out_specs = (P("grp", None), P("grp", None))
    return jax.shard_map(
        per_device, mesh=mesh, in_specs=in_specs, out_specs=out_specs, check_vma=False
    )
```

```python
import functools

import jax
import jax.numpy as jnp
from jax import lax
from jax.experimental import pallas as pl
from jax.experimental.pallas import tpu as pltpu
from jax.sharding import PartitionSpec as P

score_scale = 192.0 ** (-0.5)
neg_large = -1e30
F32 = jnp.float32
BF16 = jnp.bfloat16
MESH = pl.DeviceIdType.MESH


def for_each(low, high, body):
    if high - low <= 4:
        for i in range(low, high):
            body(i)
    else:
        lax.fori_loop(low, high, lambda i, c: (body(i), c)[1], 0)


def attend(queries, tokens, mask, width):
    scores = (
        lax.dot_general(
            queries, tokens, (((1,), (1,)), ((), ())), preferred_element_type=F32
        )
        * score_scale
    )
    top_hi, top_lo, total, weights = soften(scores, mask)
    weighted = jnp.dot(weights, tokens[:, :width], preferred_element_type=F32)
    return top_hi, top_lo, total, weighted


def soften(scores, mask):
    scores = jnp.where(mask, scores, neg_large)
    top = jnp.max(scores, axis=1, keepdims=True)
    top_hi = top.astype(BF16).astype(F32)
    rest = top - top_hi
    top_lo = (rest + jnp.abs(rest) * (2.0**-7)).astype(BF16).astype(F32)
    bound = top_hi + top_lo
    weights = jnp.where(mask, jnp.exp(scores - bound), 0.0)
    total = jnp.sum(weights, axis=1, keepdims=True)
    return top_hi, top_lo, total, weights.astype(BF16)


def up_project(latent, up_ref, heads):
    rows = latent.shape[0]
    head_of_row = lax.broadcasted_iota(jnp.int32, (rows, 1), 0) % heads
    out = None
    for head in range(heads):
        part = jnp.dot(latent, up_ref[head], preferred_element_type=F32)
        part = jnp.where(head_of_row == head, part, 0.0)
        out = part if out is None else out + part
    return out


def flatten_heads(values, heads):
    rows, width = values.shape
    head_of_row = lax.broadcasted_iota(jnp.int32, (rows, 1), 0) % heads
    wide = jnp.concatenate(
        [jnp.where(head_of_row == head, values, 0.0) for head in range(heads)], axis=1
    )
    return jnp.sum(wide.reshape(rows // heads, heads, heads * width), axis=1)


def kernel(
    n_grp,
    n_head,
    res_lengths_hbm,
    new_lengths_hbm,
    assignment_hbm,
    res_cache_hbm,
    res_query_hbm,
    new_cache_hbm,
    new_query_hbm,
    up_hbm,
    w_out_hbm,
    res_out,
    new_out,
    res_lengths,
    new_lengths,
    assignment,
    res_cache,
    res_query,
    new_cache,
    up,
    w_out,
    q_in,
    q_all,
    rep_out,
    rep_in,
    val_out,
    val_in,
    res_part,
    new_part,
    load_sem,
    r1_send,
    r1_recv,
    r2_send,
    r2_recv,
    r3_send,
    r3_recv,
    r4_send,
    r4_recv,
    r5_send,
    r5_recv,
    r6_send,
    r6_recv,
):
    grp = lax.axis_index("grp")
    head = lax.axis_index("head")
    residents, latent, slots = res_cache.shape
    heads = up.shape[0]
    width = up.shape[1]
    head_width = up.shape[2]
    requests, shard, _ = new_cache.shape
    features = w_out.shape[1]
    block_rows = n_grp * heads
    tokens = requests * shard
    splits = res_part.shape[1] // residents
    piece = features // splits

    loads = [
        pltpu.make_async_copy(src, dst, load_sem.at[i])
        for i, (src, dst) in enumerate(
            (
                (new_query_hbm.at[0], q_in.at[0]),
                (res_lengths_hbm, res_lengths),
                (new_lengths_hbm, new_lengths),
                (assignment_hbm, assignment),
                (res_query_hbm, res_query),
                (res_cache_hbm, res_cache),
                (up_hbm, up),
                (new_cache_hbm, new_cache),
                (w_out_hbm, w_out),
            )
        )
    ]
    for load in loads:
        load.start()
    load_q, load_l, load_n, load_a, load_res_q, load_res, load_up, load_new, load_w = loads

    def grp_at(off):
        return lax.rem(grp + off, n_grp)

    def head_at(off):
        return lax.rem(head + off, n_head)

    barrier = pltpu.get_barrier_semaphore()

    def greet_grp(off):
        pl.semaphore_signal(
            barrier, inc=1, device_id=(grp_at(off), head), device_id_type=MESH
        )

    def greet_head(off):
        pl.semaphore_signal(
            barrier, inc=1, device_id=(grp, head_at(off)), device_id_type=MESH
        )

    for_each(1, n_grp, greet_grp)
    for_each(1, n_head, greet_head)

    def r1(off):
        return pltpu.make_async_remote_copy(
            src_ref=new_query_hbm.at[0],
            dst_ref=q_in.at[off],
            send_sem=r1_send.at[off],
            recv_sem=r1_recv.at[off],
            device_id=(grp_at(off), head),
            device_id_type=MESH,
        )

    def r2(off):
        return pltpu.make_async_remote_copy(
            src_ref=q_all.at[0],
            dst_ref=q_all.at[off],
            send_sem=r2_send.at[off],
            recv_sem=r2_recv.at[off],
            device_id=(grp, head_at(off)),
            device_id_type=MESH,
        )

    def r3(off):
        return pltpu.make_async_remote_copy(
            src_ref=rep_out.at[off],
            dst_ref=rep_in.at[off],
            send_sem=r3_send.at[off],
            recv_sem=r3_recv.at[off],
            device_id=(grp, head_at(n_head - off)),
            device_id_type=MESH,
        )

    def r4(off):
        return pltpu.make_async_remote_copy(
            src_ref=val_out.at[off],
            dst_ref=val_in.at[off],
            send_sem=r4_send.at[off],
            recv_sem=r4_recv.at[off],
            device_id=(grp_at(n_grp - off), head),
            device_id_type=MESH,
        )

    def r5(off):
        return pltpu.make_async_remote_copy(
            src_ref=res_part.at[head],
            dst_ref=res_part.at[head],
            send_sem=r5_send.at[off],
            recv_sem=r5_recv.at[off],
            device_id=(grp, head_at(off)),
            device_id_type=MESH,
        )

    def r6(off):
        return pltpu.make_async_remote_copy(
            src_ref=new_part.at[head],
            dst_ref=new_part.at[head],
            send_sem=r6_send.at[off],
            recv_sem=r6_recv.at[off],
            device_id=(grp, head_at(off)),
            device_id_type=MESH,
        )

    pl.semaphore_wait(barrier, n_grp - 1 + n_head - 1)
    for_each(1, n_grp, lambda off: r1(off).start())

    token = lax.broadcasted_iota(jnp.int32, (1, residents * slots), 1)
    row = lax.broadcasted_iota(jnp.int32, (residents * heads, 1), 0) // heads
    live = jnp.full((1, residents * slots), -1, jnp.int32)
    load_l.wait()
    for r in range(residents):
        here = (token >= r * slots) & (token < r * slots + res_lengths[r])
        live = jnp.where(here, r, live)
    load_res_q.wait()
    load_res.wait()
    queries = res_query[...].astype(F32).reshape(residents * heads, latent).astype(BF16)
    scores = [
        jnp.dot(queries, res_cache[r], preferred_element_type=F32) * score_scale
        for r in range(residents)
    ]
    _, _, res_total, weights = soften(jnp.concatenate(scores, axis=1), row == live)
    res_weighted = None
    for r in range(residents):
        part = lax.dot_general(
            weights[:, r * slots : (r + 1) * slots],
            res_cache[r, :width, :],
            (((1,), (1,)), ((), ())),
            preferred_element_type=F32,
        )
        res_weighted = part if res_weighted is None else res_weighted + part
    res_latent = (res_weighted / res_total).astype(BF16)
    load_up.wait()
    res_values = up_project(res_latent, up, heads).astype(BF16).astype(F32)
    res_rows = flatten_heads(res_values, heads).astype(BF16)

    first = (grp * n_head + head) * shard
    token = lax.broadcasted_iota(jnp.int32, (1, tokens), 1)
    asks = jnp.full((1, tokens), -1, jnp.int32)
    load_n.wait()
    load_a.wait()
    for k in range(requests):
        here = (token >= k * shard) & (token < k * shard + (new_lengths[k] - first))
        here = here & (token < (k + 1) * shard)
        asks = jnp.where(here, assignment[k], asks)
    row = lax.broadcasted_iota(jnp.int32, (block_rows, 1), 0) // heads
    group = grp - row
    group = jnp.where(group < 0, group + n_grp, group)
    mask = group == asks

    load_q.wait()
    for_each(1, n_grp, lambda off: r1(off).wait_recv())
    q_all[0] = q_in[...].astype(F32).reshape(block_rows, latent).astype(BF16)
    for_each(1, n_head, lambda off: r2(off).start())

    load_new.wait()

    own_hi, own_lo, own_total, own_weighted = attend(
        q_all[0], new_cache[...].reshape(tokens, latent), mask, width
    )

    def answer(low, count):
        rows = count * block_rows
        top_hi, top_lo, total, weighted = attend(
            q_all[pl.ds(low, count)].reshape(rows, latent),
            new_cache[...].reshape(tokens, latent),
            jnp.concatenate([mask] * count, axis=0),
            width,
        )
        total_hi = total.astype(BF16).astype(F32)
        lane = lax.broadcasted_iota(jnp.int32, (rows, 128), 1)
        stats = jnp.where(
            lane < 64,
            jnp.where(lane < 32, top_hi, top_lo),
            jnp.where(lane < 96, total_hi, total - total_hi),
        )
        rep_out[pl.ds(low, count)] = (
            jnp.concatenate([weighted, stats], axis=1)
            .astype(BF16)
            .reshape(count, block_rows, width + 128)
        )

    if (n_head - 1) * block_rows <= 128:
        for_each(1, n_head, lambda off: r2(off).wait_recv())
        answer(1, n_head - 1)
        for_each(1, n_head, lambda off: r3(off).start())
    else:

        def answer_one(off):
            r2(off).wait_recv()
            answer(off, 1)
            r3(off).start()

        for_each(1, n_head, answer_one)

    load_w.wait()
    res_partial = jnp.dot(res_rows, w_out[...], preferred_element_type=F32)
    res_part[head] = jnp.concatenate(
        [res_partial[:, i * piece : (i + 1) * piece] for i in range(splits)], axis=0
    ).astype(BF16)
    for_each(1, n_head, lambda off: r5(off).start())

    for_each(1, n_head, lambda off: r3(off).wait_recv())
    tops = [own_hi + own_lo]
    totals = [own_total]
    for off in range(1, n_head):
        stats = rep_in[off, :, width:].astype(F32)
        tops.append(stats[:, 0:1] + stats[:, 32:33])
        totals.append(stats[:, 64:65] + stats[:, 96:97])
    top = functools.reduce(jnp.maximum, tops)
    share = jnp.exp(tops[0] - top)
    total = share * totals[0]
    summed = share * own_weighted
    for off in range(1, n_head):
        share = jnp.exp(tops[off] - top)
        total = total + share * totals[off]
        summed = summed + share * rep_in[off, :, :width].astype(F32)
    values = up_project(summed.astype(BF16), up, heads)
    lane = lax.broadcasted_iota(jnp.int32, (block_rows, 128), 1)
    stats = jnp.where(lane < 64, top, total)
    val_out[...] = jnp.concatenate([values, stats], axis=1).reshape(val_out.shape)
    for_each(1, n_grp, lambda off: r4(off).start())
    val_in[0] = val_out[0]

    for_each(1, n_head, lambda off: r5(off).wait_recv())
    res_sum = res_part[0].astype(F32)
    for rank in range(1, n_head):
        res_sum = res_sum + res_part[rank].astype(F32)
    for i in range(splits):
        res_out[:, i * piece : (i + 1) * piece] = res_sum[
            i * residents : (i + 1) * residents
        ].astype(BF16)

    for_each(1, n_grp, lambda off: r4(off).wait_recv())
    parts = val_in[...]
    tops = parts[:, :, head_width : head_width + 1]
    totals = parts[:, :, head_width + 64 : head_width + 65]
    top = jnp.max(tops, axis=0, keepdims=True)
    share = jnp.exp(tops - top)
    total = jnp.sum(share * totals, axis=0)
    values = jnp.sum(share * parts[:, :, :head_width], axis=0)
    values = (values / total).astype(BF16).astype(F32)
    new_row = flatten_heads(values, heads).astype(BF16)
    new_part[head] = jnp.dot(new_row, w_out[...], preferred_element_type=F32)
    for_each(1, n_head, lambda off: r6(off).start())
    for_each(1, n_head, lambda off: r6(off).wait_recv())
    new_sum = new_part[0]
    for rank in range(1, n_head):
        new_sum = new_sum + new_part[rank]
    new_out[...] = new_sum.astype(BF16)

    for_each(1, n_grp, lambda off: r1(off).wait_send())
    for_each(1, n_head, lambda off: r2(off).wait_send())
    for_each(1, n_head, lambda off: r3(off).wait_send())
    for_each(1, n_grp, lambda off: r4(off).wait_send())
    for_each(1, n_head, lambda off: r5(off).wait_send())
    for_each(1, n_head, lambda off: r6(off).wait_send())


def per_device(
    res_cache,
    res_lengths,
    res_query,
    new_cache,
    new_lengths,
    assignment,
    new_query,
    value_up_weight,
    w_out,
):
    n_grp = lax.axis_size("grp")
    n_head = lax.axis_size("head")
    residents = res_cache.shape[0]
    heads, width, head_width = value_up_weight.shape
    latent = res_cache.shape[2]
    res_cache = jnp.swapaxes(res_cache, 1, 2)
    features = w_out.shape[1]
    block_rows = n_grp * heads
    splits = 16 // residents
    hbm = pl.BlockSpec(memory_space=pltpu.HBM)
    vmem = pl.BlockSpec(memory_space=pltpu.VMEM)
    dma = pltpu.SemaphoreType.DMA
    grp_sems = [dma((n_grp,)), dma((n_grp,))]
    head_sems = [dma((n_head,)), dma((n_head,))]
    return pl.pallas_call(
        functools.partial(kernel, n_grp, n_head),
        out_shape=(
            jax.ShapeDtypeStruct((residents, features), BF16),
            jax.ShapeDtypeStruct((1, features), BF16),
        ),
        in_specs=[hbm] * 9,
        out_specs=(vmem, vmem),
        scratch_shapes=[
            pltpu.SMEM(res_lengths.shape, jnp.int32),
            pltpu.SMEM(new_lengths.shape, jnp.int32),
            pltpu.SMEM(assignment.shape, jnp.int32),
            pltpu.VMEM(res_cache.shape, BF16),
            pltpu.VMEM(res_query.shape, BF16),
            pltpu.VMEM(new_cache.shape, BF16),
            pltpu.VMEM(value_up_weight.shape, BF16),
            pltpu.VMEM(w_out.shape, BF16),
            pltpu.VMEM((n_grp, heads, latent), BF16),
            pltpu.VMEM((n_head, block_rows, latent), BF16),
            pltpu.VMEM((n_head, block_rows, width + 128), BF16),
            pltpu.VMEM((n_head, block_rows, width + 128), BF16),
            pltpu.VMEM((n_grp, heads, head_width + 128), F32),
            pltpu.VMEM((n_grp, heads, head_width + 128), F32),
            pltpu.VMEM((n_head, residents * splits, features // splits), BF16),
            pltpu.VMEM((n_head, 1, features), F32),
            dma((9,)),
        ]
        + grp_sems
        + head_sems * 2
        + grp_sems
        + head_sems * 2,
        compiler_params=pltpu.CompilerParams(
            collective_id=0, has_side_effects=True, vmem_limit_bytes=60 * 2**20
        ),
    )(
        res_lengths,
        new_lengths,
        assignment,
        res_cache,
        res_query,
        new_cache,
        new_query,
        value_up_weight,
        w_out,
    )


def solution(mesh):
    in_specs = (
        P("grp", None, None),
        P("grp"),
        P("grp", "head", None),
        P(None, ("grp", "head"), None),
        P(),
        P(),
        P("grp", "head", None),
        P("head", None, None),
        P("head", None),
    )
    out_specs = (P("grp", None), P("grp", None))
    return jax.shard_map(
        per_device, mesh=mesh, in_specs=in_specs, out_specs=out_specs, check_vma=False
    )
```

```python
import functools

import jax
import jax.numpy as jnp
from jax import lax
from jax.experimental import pallas as pl
from jax.experimental.pallas import tpu as pltpu
from jax.sharding import PartitionSpec as P

score_scale = 192.0 ** (-0.5)
neg_large = -1e30
F32 = jnp.float32
BF16 = jnp.bfloat16
MESH = pl.DeviceIdType.MESH


def for_each(low, high, body):
    if high - low < 32:
        for i in range(low, high):
            body(i)
    else:
        lax.fori_loop(low, high, lambda i, c: (body(i), c)[1], 0)


def attend(queries, tokens, mask, width):
    scores = (
        lax.dot_general(
            queries, tokens, (((1,), (1,)), ((), ())), preferred_element_type=F32
        )
        * score_scale
    )
    top_hi, top_lo, total, weights = soften(scores, mask)
    weighted = jnp.dot(weights, tokens[:, :width], preferred_element_type=F32)
    return top_hi, top_lo, total, weighted


def soften(scores, mask):
    scores = jnp.where(mask, scores, neg_large)
    top = jnp.max(scores, axis=1, keepdims=True)
    top_hi = top.astype(BF16).astype(F32)
    rest = top - top_hi
    top_lo = (rest + jnp.abs(rest) * (2.0**-7)).astype(BF16).astype(F32)
    bound = top_hi + top_lo
    weights = jnp.where(mask, jnp.exp(scores - bound), 0.0)
    total = jnp.sum(weights, axis=1, keepdims=True)
    return top_hi, top_lo, total, weights.astype(BF16)


def up_project(latent, up_ref, heads):
    rows = latent.shape[0]
    head_of_row = lax.broadcasted_iota(jnp.int32, (rows, 1), 0) % heads
    out = None
    for head in range(heads):
        part = jnp.dot(latent, up_ref[head], preferred_element_type=F32)
        part = jnp.where(head_of_row == head, part, 0.0)
        out = part if out is None else out + part
    return out


def flatten_heads(values, heads):
    rows, width = values.shape
    head_of_row = lax.broadcasted_iota(jnp.int32, (rows, 1), 0) % heads
    wide = jnp.concatenate(
        [jnp.where(head_of_row == head, values, 0.0) for head in range(heads)], axis=1
    )
    return jnp.sum(wide.reshape(rows // heads, heads, heads * width), axis=1)


def kernel(
    n_grp,
    n_head,
    res_lengths_hbm,
    new_lengths_hbm,
    assignment_hbm,
    res_cache_hbm,
    res_query_hbm,
    new_cache_hbm,
    new_query_hbm,
    up_hbm,
    w_out_hbm,
    res_out,
    new_out,
    res_lengths,
    new_lengths,
    assignment,
    res_cache,
    res_query,
    new_cache,
    up,
    w_out,
    q_in,
    rep_out,
    rep_in,
    res_part,
    new_part,
    load_sem,
    ask_send,
    ask_recv,
    answer_send,
    answer_recv,
    res_send,
    res_recv,
    new_send,
    new_recv,
):
    grp = lax.axis_index("grp")
    head = lax.axis_index("head")
    residents, latent, slots = res_cache.shape
    heads, width, head_width = up.shape
    requests, shard, _ = new_cache.shape
    features = w_out.shape[1]
    devices = n_grp * n_head
    tokens = requests * shard
    splits = res_part.shape[1] // residents
    piece = features // splits
    chunk = min(devices, 32)
    rows = chunk * heads

    loads = [
        pltpu.make_async_copy(src, dst, load_sem.at[i])
        for i, (src, dst) in enumerate(
            (
                (new_query_hbm.at[0], q_in.at[0]),
                (res_lengths_hbm, res_lengths),
                (new_lengths_hbm, new_lengths),
                (assignment_hbm, assignment),
                (res_query_hbm, res_query),
                (res_cache_hbm, res_cache),
                (up_hbm, up),
                (new_cache_hbm, new_cache),
                (w_out_hbm, w_out),
            )
        )
    ]
    load_q, load_l, load_n, load_a, load_res_q, load_res, load_up, load_new, load_w = loads

    def ahead(slot):
        return (
            lax.rem(grp + slot // n_head, n_grp),
            lax.rem(head + slot % n_head, n_head),
        )

    def behind(slot):
        return (
            lax.rem(grp + n_grp - slot // n_head, n_grp),
            lax.rem(head + n_head - slot % n_head, n_head),
        )

    def head_at(off):
        return (grp, lax.rem(head + off, n_head))

    barrier = pltpu.get_barrier_semaphore()

    def greet(slot):
        pl.semaphore_signal(
            barrier, inc=1, device_id=ahead(slot), device_id_type=MESH
        )

    for_each(1, devices, greet)
    for load in loads:
        load.start()

    def ask(slot):
        return pltpu.make_async_remote_copy(
            src_ref=new_query_hbm.at[0],
            dst_ref=q_in.at[slot],
            send_sem=ask_send.at[slot],
            recv_sem=ask_recv.at[slot],
            device_id=ahead(slot),
            device_id_type=MESH,
        )

    def answer(slot):
        return pltpu.make_async_remote_copy(
            src_ref=rep_out.at[slot],
            dst_ref=rep_in.at[slot],
            send_sem=answer_send.at[slot],
            recv_sem=answer_recv.at[slot],
            device_id=behind(slot),
            device_id_type=MESH,
        )

    def share_res(off):
        return pltpu.make_async_remote_copy(
            src_ref=res_part.at[head],
            dst_ref=res_part.at[head],
            send_sem=res_send.at[off],
            recv_sem=res_recv.at[off],
            device_id=head_at(off),
            device_id_type=MESH,
        )

    def share_new(off):
        return pltpu.make_async_remote_copy(
            src_ref=new_part.at[head],
            dst_ref=new_part.at[head],
            send_sem=new_send.at[off],
            recv_sem=new_recv.at[off],
            device_id=head_at(off),
            device_id_type=MESH,
        )

    pl.semaphore_wait(barrier, devices - 1)
    for_each(1, devices, lambda slot: ask(slot).start())

    token = lax.broadcasted_iota(jnp.int32, (1, residents * slots), 1)
    row = lax.broadcasted_iota(jnp.int32, (residents * heads, 1), 0) // heads
    live = jnp.full((1, residents * slots), -1, jnp.int32)
    load_l.wait()
    for r in range(residents):
        here = (token >= r * slots) & (token < r * slots + res_lengths[r])
        live = jnp.where(here, r, live)
    load_res_q.wait()
    load_res.wait()
    queries = res_query[...].astype(F32).reshape(residents * heads, latent).astype(BF16)
    scores = [
        jnp.dot(queries, res_cache[r], preferred_element_type=F32) * score_scale
        for r in range(residents)
    ]
    _, _, res_total, weights = soften(jnp.concatenate(scores, axis=1), row == live)
    res_weighted = None
    for r in range(residents):
        part = lax.dot_general(
            weights[:, r * slots : (r + 1) * slots],
            res_cache[r, :width, :],
            (((1,), (1,)), ((), ())),
            preferred_element_type=F32,
        )
        res_weighted = part if res_weighted is None else res_weighted + part
    res_latent = (res_weighted / res_total).astype(BF16)
    load_up.wait()
    res_values = up_project(res_latent, up, heads).astype(BF16).astype(F32)
    res_rows = flatten_heads(res_values, heads).astype(BF16)
    load_w.wait()
    res_partial = jnp.dot(res_rows, w_out[...], preferred_element_type=F32)
    res_part[head] = jnp.concatenate(
        [res_partial[:, i * piece : (i + 1) * piece] for i in range(splits)], axis=0
    ).astype(BF16)

    first = (grp * n_head + head) * shard
    token = lax.broadcasted_iota(jnp.int32, (1, tokens), 1)
    asks = jnp.full((1, tokens), -1, jnp.int32)
    load_n.wait()
    load_a.wait()
    for k in range(requests):
        here = (token >= k * shard) & (token < k * shard + (new_lengths[k] - first))
        here = here & (token < (k + 1) * shard)
        asks = jnp.where(here, assignment[k], asks)
    row = lax.broadcasted_iota(jnp.int32, (rows, 1), 0) // (heads * n_head)
    lane = lax.broadcasted_iota(jnp.int32, (rows, 128), 1)
    load_new.wait()
    load_q.wait()

    def attend_chunk(low):
        group = grp - row - low // n_head
        group = jnp.where(group < 0, group + n_grp, group)
        top_hi, top_lo, total, weighted = attend(
            q_in[pl.ds(low, chunk)].astype(F32).reshape(rows, latent).astype(BF16),
            new_cache[...].reshape(tokens, latent),
            group == asks,
            width,
        )
        total_hi = total.astype(BF16).astype(F32)
        stats = jnp.where(
            lane < 64,
            jnp.where(lane < 32, top_hi, top_lo),
            jnp.where(lane < 96, total_hi, total - total_hi),
        )
        rep_out[pl.ds(low, chunk)] = (
            jnp.concatenate([weighted, stats], axis=1)
            .reshape(chunk, heads, width + 128)
            .astype(BF16)
        )

    for_each(1, devices, lambda slot: ask(slot).wait_recv())
    for_each(0, devices // chunk, lambda i: attend_chunk(i * chunk))
    for_each(1, devices, lambda slot: answer(slot).start())
    for_each(1, n_head, lambda off: share_res(off).start())
    rep_in[0] = rep_out[0]
    for_each(1, devices, lambda slot: ask(slot).wait_send())

    def add_chunk(low, so_far):
        parts = rep_in[pl.ds(low, chunk)].astype(F32)
        tops = parts[:, :, width : width + 1] + parts[:, :, width + 32 : width + 33]
        totals = (
            parts[:, :, width + 64 : width + 65] + parts[:, :, width + 96 : width + 97]
        )
        top = jnp.max(tops, axis=0)
        if so_far is not None:
            top = jnp.maximum(top, so_far[0])
        share = jnp.exp(tops - top[None])
        total = jnp.sum(share * totals, axis=0)
        summed = jnp.sum(share * parts[:, :, :width], axis=0)
        if so_far is not None:
            share = jnp.exp(so_far[0] - top)
            total = total + share * so_far[1]
            summed = summed + share * so_far[2]
        return top, total, summed

    for_each(1, devices, lambda slot: answer(slot).wait_recv())
    sums = add_chunk(0, None)
    if devices > chunk:
        sums = lax.fori_loop(
            1, devices // chunk, lambda i, so_far: add_chunk(i * chunk, so_far), sums
        )
    _, total, summed = sums
    new_latent = (summed / total).astype(BF16)
    new_values = up_project(new_latent, up, heads).astype(BF16).astype(F32)
    new_row = flatten_heads(new_values, heads).astype(BF16)
    new_part[head] = jnp.dot(new_row, w_out[...], preferred_element_type=F32)
    for_each(1, n_head, lambda off: share_new(off).start())

    for_each(1, devices, lambda slot: answer(slot).wait_send())
    for_each(1, n_head, lambda off: share_res(off).wait_recv())
    res_sum = res_part[0].astype(F32)
    for rank in range(1, n_head):
        res_sum = res_sum + res_part[rank].astype(F32)
    for i in range(splits):
        res_out[:, i * piece : (i + 1) * piece] = res_sum[
            i * residents : (i + 1) * residents
        ].astype(BF16)
    for_each(1, n_head, lambda off: share_res(off).wait_send())
    for_each(1, n_head, lambda off: share_new(off).wait_recv())
    new_sum = new_part[0]
    for rank in range(1, n_head):
        new_sum = new_sum + new_part[rank]
    new_out[...] = new_sum.astype(BF16)
    for_each(1, n_head, lambda off: share_new(off).wait_send())


def write_back(res_in, new_in, res_out, new_out, sem):
    copies = [
        pltpu.make_async_copy(res_in, res_out, sem.at[0]),
        pltpu.make_async_copy(new_in, new_out, sem.at[1]),
    ]
    for copy in copies:
        copy.start()
    for copy in copies:
        copy.wait()


def per_device(
    res_cache,
    res_lengths,
    res_query,
    new_cache,
    new_lengths,
    assignment,
    new_query,
    value_up_weight,
    w_out,
):
    n_grp = lax.axis_size("grp")
    n_head = lax.axis_size("head")
    devices = n_grp * n_head
    residents = res_cache.shape[0]
    heads, width, head_width = value_up_weight.shape
    latent = res_cache.shape[2]
    res_cache = jnp.swapaxes(res_cache, 1, 2)
    features = w_out.shape[1]
    splits = 16 // residents
    hbm = pl.BlockSpec(memory_space=pltpu.HBM)
    vmem = pl.BlockSpec(memory_space=pltpu.VMEM)
    dma = pltpu.SemaphoreType.DMA
    results = pl.pallas_call(
        functools.partial(kernel, n_grp, n_head),
        out_shape=(
            pltpu.VMEM((residents, features), BF16),
            pltpu.VMEM((1, features), BF16),
        ),
        in_specs=[hbm] * 9,
        out_specs=(vmem, vmem),
        scratch_shapes=[
            pltpu.SMEM(res_lengths.shape, jnp.int32),
            pltpu.SMEM(new_lengths.shape, jnp.int32),
            pltpu.SMEM(assignment.shape, jnp.int32),
            pltpu.VMEM(res_cache.shape, BF16),
            pltpu.VMEM(res_query.shape, BF16),
            pltpu.VMEM(new_cache.shape, BF16),
            pltpu.VMEM(value_up_weight.shape, BF16),
            pltpu.VMEM(w_out.shape, BF16),
            pltpu.VMEM((devices, heads, latent), BF16),
            pltpu.VMEM((devices, heads, width + 128), BF16),
            pltpu.VMEM((devices, heads, width + 128), BF16),
            pltpu.VMEM((n_head, residents * splits, features // splits), BF16),
            pltpu.VMEM((n_head, 1, features), F32),
            dma((9,)),
        ]
        + [dma((devices,))] * 4
        + [dma((n_head,))] * 4,
        compiler_params=pltpu.CompilerParams(
            collective_id=0, has_side_effects=True, vmem_limit_bytes=60 * 2**20
        ),
    )(
        res_lengths,
        new_lengths,
        assignment,
        res_cache,
        res_query,
        new_cache,
        new_query,
        value_up_weight,
        w_out,
    )
    return pl.pallas_call(
        write_back,
        out_shape=tuple(jax.ShapeDtypeStruct(r.shape, r.dtype) for r in results),
        in_specs=[vmem, vmem],
        out_specs=(hbm, hbm),
        scratch_shapes=[dma((2,))],
    )(*results)


def solution(mesh):
    in_specs = (
        P("grp", None, None),
        P("grp"),
        P("grp", "head", None),
        P(None, ("grp", "head"), None),
        P(),
        P(),
        P("grp", "head", None),
        P("head", None, None),
        P("head", None),
    )
    out_specs = (P("grp", None), P("grp", None))
    return jax.shard_map(
        per_device, mesh=mesh, in_specs=in_specs, out_specs=out_specs, check_vma=False
    )
```

```python
import functools

import jax
import jax.numpy as jnp
from jax import lax
from jax.experimental import pallas as pl
from jax.experimental.pallas import tpu as pltpu
from jax.sharding import PartitionSpec as P

score_scale = 192.0 ** (-0.5)
neg_large = -1e30
F32 = jnp.float32
BF16 = jnp.bfloat16
MESH = pl.DeviceIdType.MESH


def for_each(low, high, body):
    if high - low < 32:
        for i in range(low, high):
            body(i)
    else:
        lax.fori_loop(low, high, lambda i, c: (body(i), c)[1], 0)


def attend(queries, tokens, mask, width):
    scores = (
        lax.dot_general(
            queries, tokens, (((1,), (1,)), ((), ())), preferred_element_type=F32
        )
        * score_scale
    )
    top_hi, top_lo, total, weights = soften(scores, mask)
    weighted = jnp.dot(weights, tokens[:, :width], preferred_element_type=F32)
    return top_hi, top_lo, total, weighted


def soften(scores, mask):
    scores = jnp.where(mask, scores, neg_large)
    top = jnp.max(scores, axis=1, keepdims=True)
    top_hi = top.astype(BF16).astype(F32)
    rest = top - top_hi
    top_lo = (rest + jnp.abs(rest) * (2.0**-7)).astype(BF16).astype(F32)
    bound = top_hi + top_lo
    weights = jnp.where(mask, jnp.exp(scores - bound), 0.0)
    total = jnp.sum(weights, axis=1, keepdims=True)
    return top_hi, top_lo, total, weights.astype(BF16)


def up_project(latent, up_ref, heads):
    rows = latent.shape[0]
    head_of_row = lax.broadcasted_iota(jnp.int32, (rows, 1), 0) % heads
    out = None
    for head in range(heads):
        part = jnp.dot(latent, up_ref[head], preferred_element_type=F32)
        part = jnp.where(head_of_row == head, part, 0.0)
        out = part if out is None else out + part
    return out


def flatten_heads(values, heads):
    rows, width = values.shape
    head_of_row = lax.broadcasted_iota(jnp.int32, (rows, 1), 0) % heads
    wide = jnp.concatenate(
        [jnp.where(head_of_row == head, values, 0.0) for head in range(heads)], axis=1
    )
    return jnp.sum(wide.reshape(rows // heads, heads, heads * width), axis=1)


def kernel(
    n_grp,
    n_head,
    res_lengths_hbm,
    new_lengths_hbm,
    assignment_hbm,
    res_cache_hbm,
    res_query_hbm,
    new_cache_hbm,
    new_query_hbm,
    up_hbm,
    w_out_hbm,
    res_out,
    new_out,
    res_lengths,
    new_lengths,
    assignment,
    res_cache,
    res_query,
    new_cache,
    up,
    w_out,
    q_in,
    rep_out,
    rep_in,
    res_part,
    new_part,
    load_sem,
    swap_sem,
    ask_send,
    ask_recv,
    answer_send,
    answer_recv,
    res_send,
    res_recv,
    new_send,
    new_recv,
):
    grp = lax.axis_index("grp")
    head = lax.axis_index("head")
    residents, latent, slots = res_cache.shape
    heads, width, head_width = up.shape
    _, requests, shard, _ = new_cache.shape
    features = w_out.shape[1]
    peers = n_grp // 2 * n_head
    sibling = grp + 1 - 2 * lax.rem(grp, 2)
    tokens = 2 * requests * shard
    splits = res_part.shape[1] // residents
    piece = features // splits
    chunk = min(peers, 16)
    rows = chunk * heads

    loads = [
        pltpu.make_async_copy(src, dst, load_sem.at[i])
        for i, (src, dst) in enumerate(
            (
                (new_query_hbm.at[0], q_in.at[0]),
                (res_lengths_hbm, res_lengths),
                (new_lengths_hbm, new_lengths),
                (assignment_hbm, assignment),
                (res_query_hbm, res_query),
                (res_cache_hbm, res_cache),
                (up_hbm, up),
                (new_cache_hbm, new_cache.at[0]),
                (w_out_hbm, w_out),
            )
        )
    ]
    load_q, load_l, load_n, load_a, load_res_q, load_res, load_up, load_new, load_w = loads

    def ahead(slot):
        return (
            lax.rem(grp + 2 * (slot // n_head), n_grp),
            lax.rem(head + slot % n_head, n_head),
        )

    def behind(slot):
        return (
            lax.rem(grp + n_grp - 2 * (slot // n_head), n_grp),
            lax.rem(head + n_head - slot % n_head, n_head),
        )

    def head_at(off):
        return (grp, lax.rem(head + off, n_head))

    barrier = pltpu.get_barrier_semaphore()

    def greet(slot):
        pl.semaphore_signal(
            barrier, inc=1, device_id=ahead(slot), device_id_type=MESH
        )

    for_each(1, peers, greet)
    pl.semaphore_signal(
        barrier, inc=1, device_id=(sibling, head), device_id_type=MESH
    )
    for load in loads:
        load.start()

    def ask(slot):
        return pltpu.make_async_remote_copy(
            src_ref=new_query_hbm.at[0],
            dst_ref=q_in.at[slot],
            send_sem=ask_send.at[slot],
            recv_sem=ask_recv.at[slot],
            device_id=ahead(slot),
            device_id_type=MESH,
        )

    def answer(slot):
        return pltpu.make_async_remote_copy(
            src_ref=rep_out.at[slot],
            dst_ref=rep_in.at[slot],
            send_sem=answer_send.at[slot],
            recv_sem=answer_recv.at[slot],
            device_id=behind(slot),
            device_id_type=MESH,
        )

    def share_res(off):
        return pltpu.make_async_remote_copy(
            src_ref=res_part.at[head],
            dst_ref=res_part.at[head],
            send_sem=res_send.at[off],
            recv_sem=res_recv.at[off],
            device_id=head_at(off),
            device_id_type=MESH,
        )

    def share_new(off):
        return pltpu.make_async_remote_copy(
            src_ref=new_part.at[head],
            dst_ref=new_part.at[head],
            send_sem=new_send.at[off],
            recv_sem=new_recv.at[off],
            device_id=head_at(off),
            device_id_type=MESH,
        )

    swap = pltpu.make_async_remote_copy(
        src_ref=new_cache_hbm,
        dst_ref=new_cache.at[1],
        send_sem=swap_sem.at[0],
        recv_sem=swap_sem.at[1],
        device_id=(sibling, head),
        device_id_type=MESH,
    )

    pl.semaphore_wait(barrier, peers)
    for_each(1, peers, lambda slot: ask(slot).start())
    swap.start()

    token = lax.broadcasted_iota(jnp.int32, (1, residents * slots), 1)
    row = lax.broadcasted_iota(jnp.int32, (residents * heads, 1), 0) // heads
    live = jnp.full((1, residents * slots), -1, jnp.int32)
    load_l.wait()
    for r in range(residents):
        here = (token >= r * slots) & (token < r * slots + res_lengths[r])
        live = jnp.where(here, r, live)
    load_res_q.wait()
    load_res.wait()
    queries = res_query[...].astype(F32).reshape(residents * heads, latent).astype(BF16)
    scores = [
        jnp.dot(queries, res_cache[r], preferred_element_type=F32) * score_scale
        for r in range(residents)
    ]
    _, _, res_total, weights = soften(jnp.concatenate(scores, axis=1), row == live)
    res_weighted = None
    for r in range(residents):
        part = lax.dot_general(
            weights[:, r * slots : (r + 1) * slots],
            res_cache[r, :width, :],
            (((1,), (1,)), ((), ())),
            preferred_element_type=F32,
        )
        res_weighted = part if res_weighted is None else res_weighted + part
    res_latent = (res_weighted / res_total).astype(BF16)
    load_up.wait()
    res_values = up_project(res_latent, up, heads).astype(BF16).astype(F32)
    res_rows = flatten_heads(res_values, heads).astype(BF16)
    load_w.wait()
    res_partial = jnp.dot(res_rows, w_out[...], preferred_element_type=F32)
    res_part[head] = jnp.concatenate(
        [res_partial[:, i * piece : (i + 1) * piece] for i in range(splits)], axis=0
    ).astype(BF16)

    token = lax.broadcasted_iota(jnp.int32, (1, tokens), 1)
    asks = jnp.full((1, tokens), -1, jnp.int32)
    load_n.wait()
    load_a.wait()
    for half, owner in enumerate((grp, sibling)):
        first = (owner * n_head + head) * shard
        for k in range(requests):
            low = (half * requests + k) * shard
            here = (token >= low) & (token < low + (new_lengths[k] - first))
            here = here & (token < low + shard)
            asks = jnp.where(here, assignment[k], asks)
    row = lax.broadcasted_iota(jnp.int32, (rows, 1), 0) // (heads * n_head) * 2
    lane = lax.broadcasted_iota(jnp.int32, (rows, 128), 1)
    load_new.wait()
    load_q.wait()
    swap.wait_recv()

    def attend_chunk(low):
        group = grp - row - low // n_head * 2
        group = jnp.where(group < 0, group + n_grp, group)
        top_hi, top_lo, total, weighted = attend(
            q_in[pl.ds(low, chunk)].astype(F32).reshape(rows, latent).astype(BF16),
            new_cache[...].reshape(tokens, latent),
            group == asks,
            width,
        )
        total_hi = total.astype(BF16).astype(F32)
        stats = jnp.where(
            lane < 64,
            jnp.where(lane < 32, top_hi, top_lo),
            jnp.where(lane < 96, total_hi, total - total_hi),
        )
        rep_out[pl.ds(low, chunk)] = (
            jnp.concatenate([weighted, stats], axis=1)
            .reshape(chunk, heads, width + 128)
            .astype(BF16)
        )

    for_each(1, peers, lambda slot: ask(slot).wait_recv())
    for_each(0, peers // chunk, lambda i: attend_chunk(i * chunk))
    for_each(1, peers, lambda slot: answer(slot).start())
    for_each(1, n_head, lambda off: share_res(off).start())
    rep_in[0] = rep_out[0]
    for_each(1, peers, lambda slot: ask(slot).wait_send())
    swap.wait_send()

    def add_chunk(low, so_far):
        parts = rep_in[pl.ds(low, chunk)].astype(F32)
        tops = parts[:, :, width : width + 1] + parts[:, :, width + 32 : width + 33]
        totals = (
            parts[:, :, width + 64 : width + 65] + parts[:, :, width + 96 : width + 97]
        )
        top = jnp.max(tops, axis=0)
        if so_far is not None:
            top = jnp.maximum(top, so_far[0])
        share = jnp.exp(tops - top[None])
        total = jnp.sum(share * totals, axis=0)
        summed = jnp.sum(share * parts[:, :, :width], axis=0)
        if so_far is not None:
            share = jnp.exp(so_far[0] - top)
            total = total + share * so_far[1]
            summed = summed + share * so_far[2]
        return top, total, summed

    for_each(1, peers, lambda slot: answer(slot).wait_recv())
    sums = add_chunk(0, None)
    if peers > chunk:
        sums = lax.fori_loop(
            1, peers // chunk, lambda i, so_far: add_chunk(i * chunk, so_far), sums
        )
    _, total, summed = sums
    new_latent = (summed / total).astype(BF16)
    new_values = up_project(new_latent, up, heads).astype(BF16).astype(F32)
    new_row = flatten_heads(new_values, heads).astype(BF16)
    new_part[head] = jnp.dot(new_row, w_out[...], preferred_element_type=F32)
    for_each(1, n_head, lambda off: share_new(off).start())

    for_each(1, peers, lambda slot: answer(slot).wait_send())
    for_each(1, n_head, lambda off: share_res(off).wait_recv())
    res_sum = res_part[0].astype(F32)
    for rank in range(1, n_head):
        res_sum = res_sum + res_part[rank].astype(F32)
    for i in range(splits):
        res_out[:, i * piece : (i + 1) * piece] = res_sum[
            i * residents : (i + 1) * residents
        ].astype(BF16)
    for_each(1, n_head, lambda off: share_res(off).wait_send())
    for_each(1, n_head, lambda off: share_new(off).wait_recv())
    new_sum = new_part[0]
    for rank in range(1, n_head):
        new_sum = new_sum + new_part[rank]
    new_out[...] = new_sum.astype(BF16)
    for_each(1, n_head, lambda off: share_new(off).wait_send())


def per_device(
    res_cache,
    res_lengths,
    res_query,
    new_cache,
    new_lengths,
    assignment,
    new_query,
    value_up_weight,
    w_out,
):
    n_grp = lax.axis_size("grp")
    n_head = lax.axis_size("head")
    peers = n_grp // 2 * n_head
    residents = res_cache.shape[0]
    heads, width, head_width = value_up_weight.shape
    latent = res_cache.shape[2]
    res_cache = jnp.swapaxes(res_cache, 1, 2)
    features = w_out.shape[1]
    splits = 16 // residents
    hbm = pl.BlockSpec(memory_space=pltpu.HBM)
    vmem = pl.BlockSpec(memory_space=pltpu.VMEM)
    dma = pltpu.SemaphoreType.DMA
    return pl.pallas_call(
        functools.partial(kernel, n_grp, n_head),
        out_shape=(
            pltpu.VMEM((residents, features), BF16),
            pltpu.VMEM((1, features), BF16),
        ),
        in_specs=[hbm] * 9,
        out_specs=(vmem, vmem),
        scratch_shapes=[
            pltpu.SMEM(res_lengths.shape, jnp.int32),
            pltpu.SMEM(new_lengths.shape, jnp.int32),
            pltpu.SMEM(assignment.shape, jnp.int32),
            pltpu.VMEM(res_cache.shape, BF16),
            pltpu.VMEM(res_query.shape, BF16),
            pltpu.VMEM((2,) + new_cache.shape, BF16),
            pltpu.VMEM(value_up_weight.shape, BF16),
            pltpu.VMEM(w_out.shape, BF16),
            pltpu.VMEM((peers, heads, latent), BF16),
            pltpu.VMEM((peers, heads, width + 128), BF16),
            pltpu.VMEM((peers, heads, width + 128), BF16),
            pltpu.VMEM((n_head, residents * splits, features // splits), BF16),
            pltpu.VMEM((n_head, 1, features), F32),
            dma((9,)),
            dma((2,)),
        ]
        + [dma((peers,))] * 4
        + [dma((n_head,))] * 4,
        compiler_params=pltpu.CompilerParams(
            collective_id=0, has_side_effects=True, vmem_limit_bytes=60 * 2**20
        ),
    )(
        res_lengths,
        new_lengths,
        assignment,
        res_cache,
        res_query,
        new_cache,
        new_query,
        value_up_weight,
        w_out,
    )


def solution(mesh):
    in_specs = (
        P("grp", None, None),
        P("grp"),
        P("grp", "head", None),
        P(None, ("grp", "head"), None),
        P(),
        P(),
        P("grp", "head", None),
        P("head", None, None),
        P("head", None),
    )
    out_specs = (P("grp", None), P("grp", None))
    return jax.shard_map(
        per_device, mesh=mesh, in_specs=in_specs, out_specs=out_specs, check_vma=False
    )
```

```python
import functools

import jax
import jax.numpy as jnp
from jax import lax
from jax.experimental import pallas as pl
from jax.experimental.pallas import tpu as pltpu
from jax.sharding import PartitionSpec as P

score_scale = 192.0 ** (-0.5)
neg_large = -1e30
F32 = jnp.float32
BF16 = jnp.bfloat16
MESH = pl.DeviceIdType.MESH


def for_each(low, high, body):
    if high - low < 32:
        for i in range(low, high):
            body(i)
    else:
        lax.fori_loop(low, high, lambda i, c: (body(i), c)[1], 0)


def attend(queries, tokens, mask, width):
    scores = (
        lax.dot_general(
            queries, tokens, (((1,), (1,)), ((), ())), preferred_element_type=F32
        )
        * score_scale
    )
    top_hi, top_lo, total, weights = soften(scores, mask)
    weighted = jnp.dot(weights, tokens[:, :width], preferred_element_type=F32)
    return top_hi, top_lo, total, weighted


def soften(scores, mask):
    scores = jnp.where(mask, scores, neg_large)
    top = jnp.max(scores, axis=1, keepdims=True)
    top_hi = top.astype(BF16).astype(F32)
    rest = top - top_hi
    top_lo = (rest + jnp.abs(rest) * (2.0**-7)).astype(BF16).astype(F32)
    bound = top_hi + top_lo
    weights = jnp.where(mask, jnp.exp(scores - bound), 0.0)
    total = jnp.sum(weights, axis=1, keepdims=True)
    return top_hi, top_lo, total, weights.astype(BF16)


def up_project(latent, up_ref, heads):
    rows = latent.shape[0]
    head_of_row = lax.broadcasted_iota(jnp.int32, (rows, 1), 0) % heads
    out = None
    for head in range(heads):
        part = jnp.dot(latent, up_ref[head], preferred_element_type=F32)
        part = jnp.where(head_of_row == head, part, 0.0)
        out = part if out is None else out + part
    return out


def flatten_heads(values, heads):
    rows, width = values.shape
    head_of_row = lax.broadcasted_iota(jnp.int32, (rows, 1), 0) % heads
    wide = jnp.concatenate(
        [jnp.where(head_of_row == head, values, 0.0) for head in range(heads)], axis=1
    )
    return jnp.sum(wide.reshape(rows // heads, heads, heads * width), axis=1)


def kernel(
    n_grp,
    n_head,
    res_lengths_hbm,
    new_lengths_hbm,
    assignment_hbm,
    res_cache_hbm,
    res_query_hbm,
    new_cache_hbm,
    new_query_hbm,
    up_hbm,
    w_out_hbm,
    res_out,
    new_out,
    res_lengths,
    new_lengths,
    assignment,
    res_cache,
    res_query,
    new_cache,
    up,
    w_out,
    q_in,
    rep_out,
    rep_in,
    res_part,
    new_part,
    load_sem,
    swap_sem,
    ask_send,
    ask_recv,
    answer_send,
    answer_recv,
    res_send,
    res_recv,
    new_send,
    new_recv,
):
    grp = lax.axis_index("grp")
    head = lax.axis_index("head")
    residents, latent, slots = res_cache.shape
    heads, width, head_width = up.shape
    _, requests, shard, _ = new_cache.shape
    features = w_out.shape[1]
    peers = n_grp // 2 * n_head
    sibling = grp + 1 - 2 * lax.rem(grp, 2)
    tokens = 2 * requests * shard
    splits = res_part.shape[1] // residents
    piece = features // splits
    chunk = min(peers, 16)
    rows = chunk * heads

    loads = [
        pltpu.make_async_copy(src, dst, load_sem.at[i])
        for i, (src, dst) in enumerate(
            (
                (new_query_hbm.at[0], q_in.at[0]),
                (res_lengths_hbm, res_lengths),
                (new_lengths_hbm, new_lengths),
                (assignment_hbm, assignment),
                (res_query_hbm, res_query),
                (res_cache_hbm, res_cache),
                (up_hbm, up),
                (new_cache_hbm, new_cache.at[0]),
                (w_out_hbm, w_out),
            )
        )
    ]
    load_q, load_l, load_n, load_a, load_res_q, load_res, load_up, load_new, load_w = loads

    def ahead(slot):
        return (
            lax.rem(grp + 2 * (slot // n_head), n_grp),
            lax.rem(head + slot % n_head, n_head),
        )

    def behind(slot):
        return (
            lax.rem(grp + n_grp - 2 * (slot // n_head), n_grp),
            lax.rem(head + n_head - slot % n_head, n_head),
        )

    def head_at(off):
        return (grp, lax.rem(head + off, n_head))

    barrier = pltpu.get_barrier_semaphore()

    def greet(slot):
        pl.semaphore_signal(
            barrier, inc=1, device_id=ahead(slot), device_id_type=MESH
        )

    for_each(1, peers, greet)
    pl.semaphore_signal(
        barrier, inc=1, device_id=(sibling, head), device_id_type=MESH
    )
    for load in loads:
        load.start()

    def ask(slot):
        return pltpu.make_async_remote_copy(
            src_ref=new_query_hbm.at[0],
            dst_ref=q_in.at[slot],
            send_sem=ask_send.at[slot],
            recv_sem=ask_recv.at[slot],
            device_id=ahead(slot),
            device_id_type=MESH,
        )

    def answer(slot):
        return pltpu.make_async_remote_copy(
            src_ref=rep_out.at[slot],
            dst_ref=rep_in.at[slot],
            send_sem=answer_send.at[slot],
            recv_sem=answer_recv.at[slot],
            device_id=behind(slot),
            device_id_type=MESH,
        )

    def share_res(off):
        return pltpu.make_async_remote_copy(
            src_ref=res_part.at[head],
            dst_ref=res_part.at[head],
            send_sem=res_send.at[off],
            recv_sem=res_recv.at[off],
            device_id=head_at(off),
            device_id_type=MESH,
        )

    def share_new(off):
        return pltpu.make_async_remote_copy(
            src_ref=new_part.at[head],
            dst_ref=new_part.at[head],
            send_sem=new_send.at[off],
            recv_sem=new_recv.at[off],
            device_id=head_at(off),
            device_id_type=MESH,
        )

    swap = pltpu.make_async_remote_copy(
        src_ref=new_cache_hbm,
        dst_ref=new_cache.at[1],
        send_sem=swap_sem.at[0],
        recv_sem=swap_sem.at[1],
        device_id=(sibling, head),
        device_id_type=MESH,
    )

    pl.semaphore_wait(barrier, peers)
    for_each(1, peers, lambda slot: ask(peers - slot).start())
    swap.start()

    token = lax.broadcasted_iota(jnp.int32, (1, residents * slots), 1)
    row = lax.broadcasted_iota(jnp.int32, (residents * heads, 1), 0) // heads
    live = jnp.full((1, residents * slots), -1, jnp.int32)
    load_l.wait()
    for r in range(residents):
        here = (token >= r * slots) & (token < r * slots + res_lengths[r])
        live = jnp.where(here, r, live)
    load_res_q.wait()
    load_res.wait()
    queries = res_query[...].astype(F32).reshape(residents * heads, latent).astype(BF16)
    scores = [
        jnp.dot(queries, res_cache[r], preferred_element_type=F32) * score_scale
        for r in range(residents)
    ]
    _, _, res_total, weights = soften(jnp.concatenate(scores, axis=1), row == live)
    res_weighted = None
    for r in range(residents):
        part = lax.dot_general(
            weights[:, r * slots : (r + 1) * slots],
            res_cache[r, :width, :],
            (((1,), (1,)), ((), ())),
            preferred_element_type=F32,
        )
        res_weighted = part if res_weighted is None else res_weighted + part
    res_latent = (res_weighted / res_total).astype(BF16)
    load_up.wait()
    res_values = up_project(res_latent, up, heads).astype(BF16).astype(F32)
    res_rows = flatten_heads(res_values, heads).astype(BF16)

    token = lax.broadcasted_iota(jnp.int32, (1, tokens), 1)
    asks = jnp.full((1, tokens), -1, jnp.int32)
    load_n.wait()
    load_a.wait()
    for half, owner in enumerate((grp, sibling)):
        first = (owner * n_head + head) * shard
        for k in range(requests):
            low = (half * requests + k) * shard
            here = (token >= low) & (token < low + (new_lengths[k] - first))
            here = here & (token < low + shard)
            asks = jnp.where(here, assignment[k], asks)
    row = lax.broadcasted_iota(jnp.int32, (rows, 1), 0) // (heads * n_head) * 2
    lane = lax.broadcasted_iota(jnp.int32, (rows, 128), 1)
    load_new.wait()
    load_q.wait()
    swap.wait_recv()

    def attend_chunk(low):
        group = grp - row - low // n_head * 2
        group = jnp.where(group < 0, group + n_grp, group)
        top_hi, top_lo, total, weighted = attend(
            q_in[pl.ds(low, chunk)].astype(F32).reshape(rows, latent).astype(BF16),
            new_cache[...].reshape(tokens, latent),
            group == asks,
            width,
        )
        total_hi = total.astype(BF16).astype(F32)
        stats = jnp.where(
            lane < 64,
            jnp.where(lane < 32, top_hi, top_lo),
            jnp.where(lane < 96, total_hi, total - total_hi),
        )
        rep_out[pl.ds(low, chunk)] = (
            jnp.concatenate([weighted, stats], axis=1)
            .reshape(chunk, heads, width + 128)
            .astype(BF16)
        )

    for_each(1, peers, lambda slot: ask(slot).wait_recv())
    for_each(0, peers // chunk, lambda i: attend_chunk(i * chunk))
    for_each(1, peers, lambda slot: answer(peers - slot).start())
    load_w.wait()
    res_partial = jnp.dot(res_rows, w_out[...], preferred_element_type=F32)
    res_part[head] = jnp.concatenate(
        [res_partial[:, i * piece : (i + 1) * piece] for i in range(splits)], axis=0
    ).astype(BF16)
    for_each(1, n_head, lambda off: share_res(off).start())
    rep_in[0] = rep_out[0]
    for_each(1, peers, lambda slot: ask(slot).wait_send())
    swap.wait_send()

    def add_chunk(low, so_far):
        parts = rep_in[pl.ds(low, chunk)].astype(F32)
        tops = parts[:, :, width : width + 1] + parts[:, :, width + 32 : width + 33]
        totals = (
            parts[:, :, width + 64 : width + 65] + parts[:, :, width + 96 : width + 97]
        )
        top = jnp.max(tops, axis=0)
        if so_far is not None:
            top = jnp.maximum(top, so_far[0])
        share = jnp.exp(tops - top[None])
        total = jnp.sum(share * totals, axis=0)
        summed = jnp.sum(share * parts[:, :, :width], axis=0)
        if so_far is not None:
            share = jnp.exp(so_far[0] - top)
            total = total + share * so_far[1]
            summed = summed + share * so_far[2]
        return top, total, summed

    for_each(1, peers, lambda slot: answer(slot).wait_recv())
    sums = add_chunk(0, None)
    if peers > chunk:
        sums = lax.fori_loop(
            1, peers // chunk, lambda i, so_far: add_chunk(i * chunk, so_far), sums
        )
    _, total, summed = sums
    new_latent = (summed / total).astype(BF16)
    new_values = up_project(new_latent, up, heads).astype(BF16).astype(F32)
    new_row = flatten_heads(new_values, heads).astype(BF16)
    new_part[head] = jnp.dot(new_row, w_out[...], preferred_element_type=F32)
    for_each(1, n_head, lambda off: share_new(off).start())

    for_each(1, peers, lambda slot: answer(slot).wait_send())
    for_each(1, n_head, lambda off: share_res(off).wait_recv())
    res_sum = res_part[0].astype(F32)
    for rank in range(1, n_head):
        res_sum = res_sum + res_part[rank].astype(F32)
    for i in range(splits):
        res_out[:, i * piece : (i + 1) * piece] = res_sum[
            i * residents : (i + 1) * residents
        ].astype(BF16)
    for_each(1, n_head, lambda off: share_res(off).wait_send())
    for_each(1, n_head, lambda off: share_new(off).wait_recv())
    new_sum = new_part[0]
    for rank in range(1, n_head):
        new_sum = new_sum + new_part[rank]
    new_out[...] = new_sum.astype(BF16)
    for_each(1, n_head, lambda off: share_new(off).wait_send())


def per_device(
    res_cache,
    res_lengths,
    res_query,
    new_cache,
    new_lengths,
    assignment,
    new_query,
    value_up_weight,
    w_out,
):
    n_grp = lax.axis_size("grp")
    n_head = lax.axis_size("head")
    peers = n_grp // 2 * n_head
    residents = res_cache.shape[0]
    heads, width, head_width = value_up_weight.shape
    latent = res_cache.shape[2]
    res_cache = jnp.swapaxes(res_cache, 1, 2)
    features = w_out.shape[1]
    splits = 16 // residents
    hbm = pl.BlockSpec(memory_space=pltpu.HBM)
    vmem = pl.BlockSpec(memory_space=pltpu.VMEM)
    dma = pltpu.SemaphoreType.DMA
    return pl.pallas_call(
        functools.partial(kernel, n_grp, n_head),
        out_shape=(
            pltpu.VMEM((residents, features), BF16),
            pltpu.VMEM((1, features), BF16),
        ),
        in_specs=[hbm] * 9,
        out_specs=(vmem, vmem),
        scratch_shapes=[
            pltpu.SMEM(res_lengths.shape, jnp.int32),
            pltpu.SMEM(new_lengths.shape, jnp.int32),
            pltpu.SMEM(assignment.shape, jnp.int32),
            pltpu.VMEM(res_cache.shape, BF16),
            pltpu.VMEM(res_query.shape, BF16),
            pltpu.VMEM((2,) + new_cache.shape, BF16),
            pltpu.VMEM(value_up_weight.shape, BF16),
            pltpu.VMEM(w_out.shape, BF16),
            pltpu.VMEM((peers, heads, latent), BF16),
            pltpu.VMEM((peers, heads, width + 128), BF16),
            pltpu.VMEM((peers, heads, width + 128), BF16),
            pltpu.VMEM((n_head, residents * splits, features // splits), BF16),
            pltpu.VMEM((n_head, 1, features), F32),
            dma((9,)),
            dma((2,)),
        ]
        + [dma((peers,))] * 4
        + [dma((n_head,))] * 4,
        compiler_params=pltpu.CompilerParams(
            collective_id=0, has_side_effects=True, vmem_limit_bytes=60 * 2**20
        ),
    )(
        res_lengths,
        new_lengths,
        assignment,
        res_cache,
        res_query,
        new_cache,
        new_query,
        value_up_weight,
        w_out,
    )


def solution(mesh):
    in_specs = (
        P("grp", None, None),
        P("grp"),
        P("grp", "head", None),
        P(None, ("grp", "head"), None),
        P(),
        P(),
        P("grp", "head", None),
        P("head", None, None),
        P("head", None),
    )
    out_specs = (P("grp", None), P("grp", None))
    return jax.shard_map(
        per_device, mesh=mesh, in_specs=in_specs, out_specs=out_specs, check_vma=False
    )
```

```python
import functools

import jax
import jax.numpy as jnp
from jax import lax
from jax.experimental import pallas as pl
from jax.experimental.pallas import tpu as pltpu
from jax.sharding import PartitionSpec as P

score_scale = 192.0 ** (-0.5)
neg_large = -1e30
F32 = jnp.float32
BF16 = jnp.bfloat16
MESH = pl.DeviceIdType.MESH


def for_each(low, high, body):
    if high - low < 32:
        for i in range(low, high):
            body(i)
    else:
        lax.fori_loop(low, high, lambda i, c: (body(i), c)[1], 0)


def attend(queries, tokens, mask, width):
    scores = (
        lax.dot_general(
            queries, tokens, (((1,), (1,)), ((), ())), preferred_element_type=F32
        )
        * score_scale
    )
    top_hi, top_lo, total, weights = soften(scores, mask)
    weighted = jnp.dot(weights, tokens[:, :width], preferred_element_type=F32)
    return top_hi, top_lo, total, weighted


def soften(scores, mask):
    scores = jnp.where(mask, scores, neg_large)
    top = jnp.max(scores, axis=1, keepdims=True)
    top_hi = top.astype(BF16).astype(F32)
    rest = top - top_hi
    top_lo = (rest + jnp.abs(rest) * (2.0**-7)).astype(BF16).astype(F32)
    bound = top_hi + top_lo
    weights = jnp.where(mask, jnp.exp(scores - bound), 0.0)
    total = jnp.sum(weights, axis=1, keepdims=True)
    return top_hi, top_lo, total, weights.astype(BF16)


def up_project(latent, up_ref, heads):
    rows = latent.shape[0]
    head_of_row = lax.broadcasted_iota(jnp.int32, (rows, 1), 0) % heads
    out = None
    for head in range(heads):
        part = jnp.dot(latent, up_ref[head], preferred_element_type=F32)
        part = jnp.where(head_of_row == head, part, 0.0)
        out = part if out is None else out + part
    return out


def flatten_heads(values, heads):
    rows, width = values.shape
    head_of_row = lax.broadcasted_iota(jnp.int32, (rows, 1), 0) % heads
    wide = jnp.concatenate(
        [jnp.where(head_of_row == head, values, 0.0) for head in range(heads)], axis=1
    )
    return jnp.sum(wide.reshape(rows // heads, heads, heads * width), axis=1)


def kernel(
    n_grp,
    n_head,
    res_lengths_hbm,
    new_lengths_hbm,
    assignment_hbm,
    res_cache_hbm,
    res_query_hbm,
    new_cache_hbm,
    new_query_hbm,
    up_hbm,
    w_out_hbm,
    res_out,
    new_out,
    res_lengths,
    new_lengths,
    assignment,
    res_cache,
    res_query,
    new_cache,
    up,
    w_out,
    q_in,
    rep_out,
    rep_in,
    res_part,
    new_part,
    load_sem,
    swap_sem,
    ask_send,
    ask_recv,
    answer_send,
    answer_recv,
    res_send,
    res_recv,
    new_send,
    new_recv,
):
    grp = lax.axis_index("grp")
    head = lax.axis_index("head")
    residents, latent, slots = res_cache.shape
    heads, width, head_width = up.shape
    _, requests, shard, _ = new_cache.shape
    features = w_out.shape[1]
    peers = n_grp // 2 * n_head
    sibling = grp + 1 - 2 * lax.rem(grp, 2)
    tokens = 2 * requests * shard
    splits = res_part.shape[1] // residents
    piece = features // splits
    chunk = min(peers, 16)
    rows = chunk * heads

    loads = [
        pltpu.make_async_copy(src, dst, load_sem.at[i])
        for i, (src, dst) in enumerate(
            (
                (new_query_hbm.at[0], q_in.at[0]),
                (res_lengths_hbm, res_lengths),
                (new_lengths_hbm, new_lengths),
                (assignment_hbm, assignment),
                (res_query_hbm, res_query),
                (res_cache_hbm, res_cache),
                (up_hbm, up),
                (new_cache_hbm, new_cache.at[0]),
                (w_out_hbm, w_out),
            )
        )
    ]
    load_q, load_l, load_n, load_a, load_res_q, load_res, load_up, load_new, load_w = loads

    def ahead(slot):
        return (
            lax.rem(grp + 2 * (slot // n_head), n_grp),
            lax.rem(head + slot % n_head, n_head),
        )

    def behind(slot):
        return (
            lax.rem(grp + n_grp - 2 * (slot // n_head), n_grp),
            lax.rem(head + n_head - slot % n_head, n_head),
        )

    def head_at(off):
        return (grp, lax.rem(head + off, n_head))

    barrier = pltpu.get_barrier_semaphore()

    def greet(slot):
        pl.semaphore_signal(
            barrier, inc=1, device_id=ahead(slot), device_id_type=MESH
        )

    for_each(1, peers, lambda slot: greet(peers - slot))
    pl.semaphore_signal(
        barrier, inc=1, device_id=(sibling, head), device_id_type=MESH
    )
    for load in loads:
        load.start()

    def ask(slot):
        return pltpu.make_async_remote_copy(
            src_ref=new_query_hbm.at[0],
            dst_ref=q_in.at[slot],
            send_sem=ask_send.at[slot],
            recv_sem=ask_recv.at[slot],
            device_id=ahead(slot),
            device_id_type=MESH,
        )

    def answer(slot):
        return pltpu.make_async_remote_copy(
            src_ref=rep_out.at[slot],
            dst_ref=rep_in.at[slot],
            send_sem=answer_send.at[slot],
            recv_sem=answer_recv.at[slot],
            device_id=behind(slot),
            device_id_type=MESH,
        )

    def share_res(off):
        return pltpu.make_async_remote_copy(
            src_ref=res_part.at[head],
            dst_ref=res_part.at[head],
            send_sem=res_send.at[off],
            recv_sem=res_recv.at[off],
            device_id=head_at(off),
            device_id_type=MESH,
        )

    def share_new(off):
        return pltpu.make_async_remote_copy(
            src_ref=new_part.at[head],
            dst_ref=new_part.at[head],
            send_sem=new_send.at[off],
            recv_sem=new_recv.at[off],
            device_id=head_at(off),
            device_id_type=MESH,
        )

    swap = pltpu.make_async_remote_copy(
        src_ref=new_cache_hbm,
        dst_ref=new_cache.at[1],
        send_sem=swap_sem.at[0],
        recv_sem=swap_sem.at[1],
        device_id=(sibling, head),
        device_id_type=MESH,
    )

    pl.semaphore_wait(barrier, peers)
    for_each(1, peers, lambda slot: ask(peers - slot).start())
    swap.start()

    token = lax.broadcasted_iota(jnp.int32, (1, residents * slots), 1)
    row = lax.broadcasted_iota(jnp.int32, (residents * heads, 1), 0) // heads
    live = jnp.full((1, residents * slots), -1, jnp.int32)
    load_l.wait()
    for r in range(residents):
        here = (token >= r * slots) & (token < r * slots + res_lengths[r])
        live = jnp.where(here, r, live)
    load_res_q.wait()
    load_res.wait()
    queries = res_query[...].astype(F32).reshape(residents * heads, latent).astype(BF16)
    scores = [
        jnp.dot(queries, res_cache[r], preferred_element_type=F32) * score_scale
        for r in range(residents)
    ]
    _, _, res_total, weights = soften(jnp.concatenate(scores, axis=1), row == live)
    res_weighted = None
    for r in range(residents):
        part = lax.dot_general(
            weights[:, r * slots : (r + 1) * slots],
            res_cache[r, :width, :],
            (((1,), (1,)), ((), ())),
            preferred_element_type=F32,
        )
        res_weighted = part if res_weighted is None else res_weighted + part
    res_latent = (res_weighted / res_total).astype(BF16)
    load_up.wait()
    res_values = up_project(res_latent, up, heads).astype(BF16).astype(F32)
    res_rows = flatten_heads(res_values, heads).astype(BF16)

    token = lax.broadcasted_iota(jnp.int32, (1, tokens), 1)
    asks = jnp.full((1, tokens), -1, jnp.int32)
    load_n.wait()
    load_a.wait()
    for half, owner in enumerate((grp, sibling)):
        first = (owner * n_head + head) * shard
        for k in range(requests):
            low = (half * requests + k) * shard
            here = (token >= low) & (token < low + (new_lengths[k] - first))
            here = here & (token < low + shard)
            asks = jnp.where(here, assignment[k], asks)
    row = lax.broadcasted_iota(jnp.int32, (rows, 1), 0) // (heads * n_head) * 2
    lane = lax.broadcasted_iota(jnp.int32, (rows, 128), 1)
    load_new.wait()
    load_q.wait()
    swap.wait_recv()

    def attend_chunk(low):
        group = grp - row - low // n_head * 2
        group = jnp.where(group < 0, group + n_grp, group)
        top_hi, top_lo, total, weighted = attend(
            q_in[pl.ds(low, chunk)].astype(F32).reshape(rows, latent).astype(BF16),
            new_cache[...].reshape(tokens, latent),
            group == asks,
            width,
        )
        total_hi = total.astype(BF16).astype(F32)
        stats = jnp.where(
            lane < 64,
            jnp.where(lane < 32, top_hi, top_lo),
            jnp.where(lane < 96, total_hi, total - total_hi),
        )
        rep_out[pl.ds(low, chunk)] = (
            jnp.concatenate([weighted, stats], axis=1)
            .reshape(chunk, heads, width + 128)
            .astype(BF16)
        )

    for_each(1, peers, lambda slot: ask(slot).wait_recv())
    for_each(0, peers // chunk, lambda i: attend_chunk(i * chunk))
    for_each(1, peers, lambda slot: answer(peers - slot).start())
    load_w.wait()
    res_partial = jnp.dot(res_rows, w_out[...], preferred_element_type=F32)
    res_part[head] = jnp.concatenate(
        [res_partial[:, i * piece : (i + 1) * piece] for i in range(splits)], axis=0
    ).astype(BF16)
    for_each(1, n_head, lambda off: share_res(off).start())
    rep_in[0] = rep_out[0]
    for_each(1, peers, lambda slot: ask(slot).wait_send())
    swap.wait_send()

    def add_chunk(low, so_far):
        parts = rep_in[pl.ds(low, chunk)].astype(F32)
        tops = parts[:, :, width : width + 1] + parts[:, :, width + 32 : width + 33]
        totals = (
            parts[:, :, width + 64 : width + 65] + parts[:, :, width + 96 : width + 97]
        )
        top = jnp.max(tops, axis=0)
        if so_far is not None:
            top = jnp.maximum(top, so_far[0])
        share = jnp.exp(tops - top[None])
        total = jnp.sum(share * totals, axis=0)
        summed = jnp.sum(share * parts[:, :, :width], axis=0)
        if so_far is not None:
            share = jnp.exp(so_far[0] - top)
            total = total + share * so_far[1]
            summed = summed + share * so_far[2]
        return top, total, summed

    for_each(1, peers, lambda slot: answer(slot).wait_recv())
    sums = add_chunk(0, None)
    if peers > chunk:
        sums = lax.fori_loop(
            1, peers // chunk, lambda i, so_far: add_chunk(i * chunk, so_far), sums
        )
    _, total, summed = sums
    new_latent = (summed / total).astype(BF16)
    new_values = up_project(new_latent, up, heads).astype(BF16).astype(F32)
    new_row = flatten_heads(new_values, heads).astype(BF16)
    new_part[head] = jnp.dot(new_row, w_out[...], preferred_element_type=F32)
    for_each(1, n_head, lambda off: share_new(n_head - off).start())

    for_each(1, peers, lambda slot: answer(slot).wait_send())
    for_each(1, n_head, lambda off: share_res(off).wait_recv())
    res_sum = res_part[0].astype(F32)
    for rank in range(1, n_head):
        res_sum = res_sum + res_part[rank].astype(F32)
    for i in range(splits):
        res_out[:, i * piece : (i + 1) * piece] = res_sum[
            i * residents : (i + 1) * residents
        ].astype(BF16)
    for_each(1, n_head, lambda off: share_res(off).wait_send())
    for_each(1, n_head, lambda off: share_new(off).wait_recv())
    new_sum = new_part[0]
    for rank in range(1, n_head):
        new_sum = new_sum + new_part[rank]
    new_out[...] = new_sum.astype(BF16)
    for_each(1, n_head, lambda off: share_new(off).wait_send())


def per_device(
    res_cache,
    res_lengths,
    res_query,
    new_cache,
    new_lengths,
    assignment,
    new_query,
    value_up_weight,
    w_out,
):
    n_grp = lax.axis_size("grp")
    n_head = lax.axis_size("head")
    peers = n_grp // 2 * n_head
    residents = res_cache.shape[0]
    heads, width, head_width = value_up_weight.shape
    latent = res_cache.shape[2]
    res_cache = jnp.swapaxes(res_cache, 1, 2)
    features = w_out.shape[1]
    splits = 16 // residents
    hbm = pl.BlockSpec(memory_space=pltpu.HBM)
    vmem = pl.BlockSpec(memory_space=pltpu.VMEM)
    dma = pltpu.SemaphoreType.DMA
    return pl.pallas_call(
        functools.partial(kernel, n_grp, n_head),
        out_shape=(
            pltpu.VMEM((residents, features), BF16),
            pltpu.VMEM((1, features), BF16),
        ),
        in_specs=[hbm] * 9,
        out_specs=(vmem, vmem),
        scratch_shapes=[
            pltpu.SMEM(res_lengths.shape, jnp.int32),
            pltpu.SMEM(new_lengths.shape, jnp.int32),
            pltpu.SMEM(assignment.shape, jnp.int32),
            pltpu.VMEM(res_cache.shape, BF16),
            pltpu.VMEM(res_query.shape, BF16),
            pltpu.VMEM((2,) + new_cache.shape, BF16),
            pltpu.VMEM(value_up_weight.shape, BF16),
            pltpu.VMEM(w_out.shape, BF16),
            pltpu.VMEM((peers, heads, latent), BF16),
            pltpu.VMEM((peers, heads, width + 128), BF16),
            pltpu.VMEM((peers, heads, width + 128), BF16),
            pltpu.VMEM((n_head, residents * splits, features // splits), BF16),
            pltpu.VMEM((n_head, 1, features), F32),
            dma((9,)),
            dma((2,)),
        ]
        + [dma((peers,))] * 4
        + [dma((n_head,))] * 4,
        compiler_params=pltpu.CompilerParams(
            collective_id=0, has_side_effects=True, vmem_limit_bytes=60 * 2**20
        ),
    )(
        res_lengths,
        new_lengths,
        assignment,
        res_cache,
        res_query,
        new_cache,
        new_query,
        value_up_weight,
        w_out,
    )


def solution(mesh):
    in_specs = (
        P("grp", None, None),
        P("grp"),
        P("grp", "head", None),
        P(None, ("grp", "head"), None),
        P(),
        P(),
        P("grp", "head", None),
        P("head", None, None),
        P("head", None),
    )
    out_specs = (P("grp", None), P("grp", None))
    return jax.shard_map(
        per_device, mesh=mesh, in_specs=in_specs, out_specs=out_specs, check_vma=False
    )
```
